32 devices in a mesh: crop: 2 (over x), row: 4 (over y, core), col: 4 (over z).
Axes of the slice: x: 2, y: 2, z: 4, core: 2. Of those that a mesh axis runs over, the one named last changes fastest.
Arguments:
- alignment_activations: bfloat16 [128, 256, 256], P('crop', 'row'), parts along dimension 0, may hold values from -12 to 12
- sequence_presence_flags: int32 [128, 256], P('crop'), parts along dimension 0, may hold values 0 or 1
- residue_padding_mask: int32 [512], P('crop'), parts along dimension 0, may hold values 0 or 1
- left_weight: bfloat16 [256, 32], replicated, may hold values from -0.375 to 0.375
- right_weight: bfloat16 [256, 32], replicated, may hold values from -0.375 to 0.375
- output_weight: bfloat16 [1024, 128], replicated, may hold values from -0.1875 to 0.1875
- cotangent: bfloat16 [512, 256, 128], P(('crop', 'row'), 'col'), parts along dimension 0, may hold values from -6 to 6
Outputs:
- pair_state_update: bfloat16 [512, 256, 128], P(('crop', 'row'), 'col'), parts along dimension 0
- alignment_gradient: bfloat16 [128, 256, 256], P('crop', 'row'), parts along dimension 0
- grad_w_out: float32 [2048, 128], P(('crop', 'row', 'col')), parts along dimension 0
- left_weight_gradient: float32 [512, 32], P('crop'), parts along dimension 0
- right_weight_gradient: float32 [512, 32], P('crop'), parts along dimension 0
The draws below stay inside these ranges and needn't reach their ends.
There are 2 independent parts, one for each index of `crop`. The reference program is written for one: setup_inputs(seed, part) draws one part's arguments, and reference() takes and returns one part's arrays. A program takes and returns all parts, laid end to end along the dimension named above; an argument that names none is the same for every part. Nothing has to cross between parts.
All inputs are finite; a program needn't handle non-finite values.
Results may differ from the reference program's by a relative error of at most 0.0075.
Values may be sent and summed in bfloat16 or wider, within the bound.
A program may use at most 128 MiB of HBM per device.

```python
import math
import jax
import jax.numpy as jnp
from jax import lax

SEQUENCE_NUMBER = 64
SEQUENCE_WIDTH = 256
PROJECTION_WIDTH = 32
CONTACT_WIDTH = 128
CHAIN_LENGTH = 256


def draw_alignment_activations(key, part):
    key = jax.random.fold_in(key, 11)
    key_common, coarse_random_seed = jax.random.split(key, 2)
    common = jax.random.normal(key_common, (CHAIN_LENGTH, SEQUENCE_WIDTH), jnp.float32)
    coarse_values = jax.random.normal(coarse_random_seed, (SEQUENCE_NUMBER, CHAIN_LENGTH, SEQUENCE_WIDTH), jnp.float32)
    values = 0.5 * common[None, :, :] + coarse_values
    return jnp.clip(values, -12.0, 12.0).astype(jnp.bfloat16)


def place_ends(entries, stream_key, low, top_value):
    shape = entries.shape
    place = [jax.random.randint(jax.random.fold_in(stream_key, axis), (), 0, shape[axis]) for axis in range(len(shape))]
    entries = entries.at[tuple(place)].set(low)
    longest = shape.index(max(shape))
    place[longest] = (place[longest] + 1) % shape[longest]
    return entries.at[tuple(place)].set(top_value)


def block_scale(key, shape, pieces, low, top_value):
    def one(dim, shards_of):
        heights = jax.random.uniform(jax.random.fold_in(jax.random.fold_in(key, 6), dim), (shards_of,), jnp.float32, low / len(pieces), top_value / len(pieces))
        return jnp.repeat(jnp.exp(heights), shape[dim] // shards_of).reshape((-1,) + (1,) * (len(shape) - dim - 1))

    gain = one(*pieces[0])
    for cut in pieces[1:]:
        gain = gain * one(*cut)
    return gain


def scatter_about(key, extent, deviation, limit, shards=(), kind=jnp.bfloat16):
    gain = block_scale(key, extent, shards, -0.22, 0.18) if shards else 1.0
    drawn = jax.random.normal(key, extent, jnp.float32) * deviation * gain
    return jnp.minimum(jnp.maximum(drawn, -limit), limit).astype(kind)


def setup_inputs(seed: int = 0, part: int = 0) -> dict:
    streams_of = jax.random.split(jax.random.key(seed), 8)
    own_keys = jax.random.split(jax.random.fold_in(streams_of[7], part), 8)
    return {
        "alignment_activations": draw_alignment_activations(jax.random.fold_in(jax.random.fold_in(streams_of[7], part), 71), part),
        "sequence_presence_flags": place_ends((jax.random.randint(own_keys[1], (SEQUENCE_NUMBER, CHAIN_LENGTH), 0, 4) < 3).astype(jnp.int32), jax.random.fold_in(own_keys[1], 1), 0, 1),
        "residue_padding_mask": place_ends((jax.random.randint(own_keys[2], (CHAIN_LENGTH,), 0, 8) < 7).astype(jnp.int32), jax.random.fold_in(own_keys[2], 1), 0, 1),
        "left_weight": scatter_about(streams_of[3], (SEQUENCE_WIDTH, PROJECTION_WIDTH), SEQUENCE_WIDTH ** -0.5, 0.375),
        "right_weight": scatter_about(streams_of[4], (SEQUENCE_WIDTH, PROJECTION_WIDTH), SEQUENCE_WIDTH ** -0.5, 0.375),
        "output_weight": scatter_about(streams_of[5], (PROJECTION_WIDTH * PROJECTION_WIDTH, CONTACT_WIDTH), (PROJECTION_WIDTH * PROJECTION_WIDTH) ** -0.5, 0.1875),
        "cotangent": scatter_about(own_keys[6], (CHAIN_LENGTH, CHAIN_LENGTH, CONTACT_WIDTH), 1.0, 6.0, ((0, 4), (1, 4))),
    }


norm_eps = 1e-05

def layer_normalize(values):
    floats = values.astype(jnp.float32)
    average = lax.optimization_barrier(jnp.mean(floats, -1, keepdims=True))
    centred = floats - average
    variance = lax.optimization_barrier(jnp.mean(centred * centred, -1, keepdims=True))
    inverse_deviation = lax.rsqrt(variance + norm_eps)
    return (centred * inverse_deviation, inverse_deviation)

def round_half(values):
    return lax.optimization_barrier(values.astype(jnp.bfloat16)).astype(jnp.float32)

def reference(alignment_activations, sequence_presence_flags, residue_padding_mask, left_weight, right_weight, output_weight, cotangent):
    unit_alignment, inverse_deviation = layer_normalize(alignment_activations)
    normalized_input = unit_alignment.astype(jnp.bfloat16)
    active_mask = (sequence_presence_flags * residue_padding_mask[None, :]).astype(jnp.float32)
    normed_f = normalized_input.astype(jnp.float32)
    left_act = (jnp.einsum('snd,dc->snc', normed_f, left_weight.astype(jnp.float32)) * active_mask[..., None]).astype(jnp.bfloat16)
    right_act = (jnp.einsum('snd,dc->snc', normed_f, right_weight.astype(jnp.float32)) * active_mask[..., None]).astype(jnp.bfloat16)
    pair_count = jnp.dot(active_mask.T, active_mask, precision=lax.Precision.HIGHEST)
    divisor = jnp.maximum(pair_count, 1.0)
    left_f = left_act.astype(jnp.float32)
    right_f = right_act.astype(jnp.float32)
    out_f = output_weight.astype(jnp.float32)
    block_rows = math.gcd(CHAIN_LENGTH, 32)

    def block_step(totals, first_row):
        output_gradient, right_acc = totals
        left_block = lax.dynamic_slice_in_dim(left_f, first_row, block_rows, 1)
        block_div = lax.dynamic_slice_in_dim(divisor, first_row, block_rows, 0)[..., None]
        cot_block = lax.dynamic_slice_in_dim(cotangent, first_row, block_rows, 0).astype(jnp.float32)
        outer_prod = round_half(jnp.einsum('sic,sje->ijce', left_block, right_f)).reshape(block_rows, CHAIN_LENGTH, PROJECTION_WIDTH * PROJECTION_WIDTH)
        pair_block = (jnp.einsum('ijk,kz->ijz', outer_prod, out_f) / block_div).astype(jnp.bfloat16)
        scaled = round_half(cot_block / block_div)
        output_gradient = output_gradient + jnp.einsum('ijk,ijz->kz', outer_prod, scaled)
        grad_outer = round_half(jnp.einsum('ijz,kz->ijk', scaled, out_f)).reshape(block_rows, CHAIN_LENGTH, PROJECTION_WIDTH, PROJECTION_WIDTH)
        left_grad = jnp.einsum('ijce,sje->sic', grad_outer, right_f)
        right_acc = right_acc + jnp.einsum('ijce,sic->sje', grad_outer, left_block)
        return ((output_gradient, right_acc), (pair_block, left_grad))
    starts = jnp.arange(CHAIN_LENGTH // block_rows, dtype=jnp.int32) * block_rows
    starting_value = (jnp.zeros((PROJECTION_WIDTH * PROJECTION_WIDTH, CONTACT_WIDTH), jnp.float32), jnp.zeros((SEQUENCE_NUMBER, CHAIN_LENGTH, PROJECTION_WIDTH), jnp.float32))
    (output_gradient, right_acc), (pair_blocks, first_factor_tiles) = lax.scan(block_step, starting_value, starts)
    pair_state_update = pair_blocks.reshape(CHAIN_LENGTH, CHAIN_LENGTH, CONTACT_WIDTH)
    first_factor_accrued = jnp.transpose(first_factor_tiles, (1, 0, 2, 3)).reshape(SEQUENCE_NUMBER, CHAIN_LENGTH, PROJECTION_WIDTH)
    grad_left = (first_factor_accrued * active_mask[..., None]).astype(jnp.bfloat16)
    grad_right = (right_acc * active_mask[..., None]).astype(jnp.bfloat16)
    gleft_f = grad_left.astype(jnp.float32)
    gright_f = grad_right.astype(jnp.float32)
    left_weight_gradient = jnp.einsum('snd,snc->dc', normed_f, gleft_f) / CHAIN_LENGTH
    right_weight_gradient = jnp.einsum('snd,snc->dc', normed_f, gright_f) / CHAIN_LENGTH
    normalized_gradient = jnp.einsum('snc,dc->snd', gleft_f, left_weight.astype(jnp.float32)) + jnp.einsum('snc,dc->snd', gright_f, right_weight.astype(jnp.float32))
    centered_gradient = normalized_gradient - lax.optimization_barrier(jnp.mean(normalized_gradient, -1, keepdims=True)) - unit_alignment * lax.optimization_barrier(jnp.mean(normalized_gradient * unit_alignment, -1, keepdims=True))
    alignment_gradient = (inverse_deviation * centered_gradient).astype(jnp.bfloat16)
    return (pair_state_update, alignment_gradient, output_gradient / CHAIN_LENGTH, left_weight_gradient, right_weight_gradient)
```

```python
import functools

import jax
import jax.numpy as jnp
from jax import lax
from jax.experimental import pallas as pl
from jax.experimental.pallas import tpu as pltpu
from jax.sharding import PartitionSpec as P

norm_eps = 1e-05
MESH = pl.DeviceIdType.MESH
NT = (((1,), (1,)), ((), ()))
TN = (((0,), (0,)), ((), ()))
VMEM = pl.BlockSpec(memory_space=pltpu.VMEM)
f32 = jnp.float32
bf16 = jnp.bfloat16


def layer_normalize(values):
    floats = values.astype(jnp.float32)
    average = jnp.mean(floats, -1, keepdims=True)
    centred = floats - average
    variance = jnp.mean(centred * centred, -1, keepdims=True)
    inverse_deviation = lax.rsqrt(variance + norm_eps)
    return (centred * inverse_deviation, inverse_deviation)


def spread_kernel(row_devs, ratio, own_ref, out_ref, send_sem, recv_sem):
    r = lax.axis_index("row")
    c = lax.axis_index("col")
    barrier = pltpu.get_barrier_semaphore()
    for d in range(1, row_devs):
        pl.semaphore_signal(
            barrier, inc=1, device_id={"row": lax.rem(r + d, row_devs)}, device_id_type=MESH
        )
    pl.semaphore_wait(barrier, row_devs - 1)

    def copy(k, d):
        return pltpu.make_async_remote_copy(
            src_ref=own_ref,
            dst_ref=out_ref.at[k],
            send_sem=send_sem.at[d],
            recv_sem=recv_sem.at[k],
            device_id={"row": lax.rem(r + d, row_devs)},
            device_id_type=MESH,
        )

    for k in range(ratio):

        @pl.when(c * ratio + k == r)
        def _():
            for d in range(1, row_devs):
                copy(k, d).start()
            out_ref[k] = own_ref[...]

    for k in range(ratio):

        @pl.when(c * ratio + k != r)
        def _():
            copy(k, 1).wait_recv()

        @pl.when(c * ratio + k == r)
        def _():
            for d in range(1, row_devs):
                copy(k, d).wait_send()


def spread_right(own, row_devs, ratio):
    return pl.pallas_call(
        functools.partial(spread_kernel, row_devs, ratio),
        out_shape=jax.ShapeDtypeStruct((ratio,) + own.shape, own.dtype),
        in_specs=[VMEM],
        out_specs=VMEM,
        scratch_shapes=[
            pltpu.SemaphoreType.DMA((row_devs,)),
            pltpu.SemaphoreType.DMA((ratio,)),
        ],
        compiler_params=pltpu.CompilerParams(collective_id=0, has_side_effects=True),
        name="spread_right",
    )(own)


def pair_kernel(
    ib,
    width,
    per,
    left_ref,
    right_ref,
    div_ref,
    cot_ref,
    wst_ref,
    wst2_ref,
    live_left_ref,
    live_right_ref,
    pair_ref,
    gleft_ref,
    gright_ref,
    gw_ref,
    x_ref,
    s_ref,
    gp_ref,
    gr_acc,
    gw_acc,
):
    step = pl.program_id(0)
    cols = cot_ref.shape[1]
    z = cot_ref.shape[2]
    tile = per * cols
    groups = width // per

    @pl.when(step == 0)
    def _():
        s_ref[...] = jnp.zeros_like(s_ref)
        gr_acc[...] = jnp.zeros_like(gr_acc)
        gw_acc[...] = jnp.zeros_like(gw_acc)

    left = left_ref[...]
    for g in range(groups):
        part = lax.dot_general(
            left, right_ref[:, g * tile : (g + 1) * tile], TN, preferred_element_type=f32
        ).astype(bf16)
        for i in range(ib):
            x_ref[g * width : (g + 1) * width, i * tile : (i + 1) * tile] = part[
                i * width : (i + 1) * width
            ]
    inverse = 1.0 / div_ref[0]
    for i in range(ib):
        scaled = (cot_ref[i].astype(f32) * inverse[:, i : i + 1]).astype(bf16)
        for p in range(per):
            s_ref[i * tile + p * cols : i * tile + (p + 1) * cols, p * z : (p + 1) * z] = scaled

    lanes = lax.broadcasted_iota(jnp.int32, (z, tile), 1)
    for i in range(ib):
        sl = slice(i * tile, (i + 1) * tile)
        y = jnp.dot(wst_ref[...], x_ref[:, sl], preferred_element_type=f32)
        picked = y[:z]
        for p in range(1, per):
            picked = jnp.where(lanes < p * cols, picked, y[p * z : (p + 1) * z])
        turned = picked.T
        total = turned[:cols]
        for p in range(1, per):
            total = total + turned[p * cols : (p + 1) * cols]
        pair_ref[i] = (total * inverse[:, i : i + 1]).astype(bf16)

    gw_acc[...] += jnp.dot(x_ref[...], s_ref[...], preferred_element_type=f32)

    for g in range(groups):
        rows = slice(g * width, (g + 1) * width)
        go = lax.dot_general(wst2_ref[rows], s_ref[...], NT, preferred_element_type=f32).astype(bf16)
        for i in range(ib):
            gp_ref[i * width : (i + 1) * width, g * tile : (g + 1) * tile] = go[
                :, i * tile : (i + 1) * tile
            ]
    gl = lax.dot_general(right_ref[...], gp_ref[...], NT, preferred_element_type=f32)
    gleft_ref[...] = (gl * live_left_ref[...].astype(f32)).astype(bf16)
    gr_acc[...] += jnp.dot(left, gp_ref[...], preferred_element_type=f32)

    @pl.when(step == pl.num_programs(0) - 1)
    def _():
        gright_ref[...] = (gr_acc[...] * live_right_ref[...].astype(f32)).astype(bf16)
        gw_ref[...] = gw_acc[...].astype(bf16)


def pair_block(left, right, divisor, cotangent, weight, live_left, live_right, width):
    rows, cols, z = cotangent.shape
    seqs = left.shape[0]
    ib = 8
    steps = rows // ib
    per = max(1, 128 // cols)
    tile = per * cols
    groups = width // per
    wst2 = weight.reshape(width, groups, per, z).transpose(1, 0, 2, 3)
    wst2 = wst2.reshape(groups * width, per * z)
    div = divisor.reshape(steps, ib, cols).transpose(0, 2, 1)
    whole = lambda shape: pl.BlockSpec(shape, lambda i: (0,) * len(shape))
    return pl.pallas_call(
        functools.partial(pair_kernel, ib, width, per),
        grid=(steps,),
        out_shape=(
            jax.ShapeDtypeStruct((rows, cols, z), bf16),
            jax.ShapeDtypeStruct((seqs, rows * width), bf16),
            jax.ShapeDtypeStruct((seqs, cols * width), bf16),
            jax.ShapeDtypeStruct((groups * width, per * z), bf16),
        ),
        in_specs=[
            pl.BlockSpec((seqs, ib * width), lambda i: (0, i)),
            whole((seqs, cols * width)),
            pl.BlockSpec((1, cols, ib), lambda i: (i, 0, 0)),
            pl.BlockSpec((ib, cols, z), lambda i: (i, 0, 0)),
            whole((per * z, groups * width)),
            whole((groups * width, per * z)),
            pl.BlockSpec((seqs, ib * width), lambda i: (0, i)),
            whole((seqs, cols * width)),
        ],
        out_specs=(
            pl.BlockSpec((ib, cols, z), lambda i: (i, 0, 0)),
            pl.BlockSpec((seqs, ib * width), lambda i: (0, i)),
            whole((seqs, cols * width)),
            whole((groups * width, per * z)),
        ),
        scratch_shapes=[
            pltpu.VMEM((groups * width, ib * tile), bf16),
            pltpu.VMEM((ib * tile, per * z), bf16),
            pltpu.VMEM((ib * width, groups * tile), bf16),
            pltpu.VMEM((seqs, cols * width), f32),
            pltpu.VMEM((groups * width, per * z), f32),
        ],
        compiler_params=pltpu.CompilerParams(vmem_limit_bytes=48 * 1024 * 1024),
        name="pair_block",
    )(left, right, div, cotangent, wst2.T, wst2, live_left, live_right)


def sums_kernel(
    row_devs,
    col_devs,
    ratio,
    scale,
    gl_ref,
    gr_ref,
    gw_ref,
    out_l,
    out_r,
    out_w,
    buf_l,
    buf_r,
    buf_w,
    done_l,
    done_r,
    l_send,
    l_recv,
    r_send,
    r_recv,
    w_send,
    w_recv,
    l2_send,
    l2_recv,
    r2_send,
    r2_recv,
):
    r = lax.axis_index("row")
    c = lax.axis_index("col")
    count = row_devs * col_devs
    me = r * col_devs + c

    def place(d):
        peer = lax.rem(me + d, count)
        return peer, {"row": peer // col_devs, "col": lax.rem(peer, col_devs)}

    barrier = pltpu.get_barrier_semaphore()
    for d in range(1, count):
        pl.semaphore_signal(barrier, inc=1, device_id=place(d)[1], device_id_type=MESH)
    pl.semaphore_wait(barrier, count - 1)

    def remote(src, dst, send, recv, where):
        return pltpu.make_async_remote_copy(
            src_ref=src,
            dst_ref=dst,
            send_sem=send,
            recv_sem=recv,
            device_id=where,
            device_id_type=MESH,
        )

    lefts, rights, outs = [], [], []
    for d in range(1, col_devs):
        peer = lax.rem(c + d, col_devs)
        lefts.append(
            remote(
                gl_ref.at[peer], buf_l.at[d - 1], l_send.at[d - 1], l_recv.at[d - 1], {"col": peer}
            )
        )
    for d in range(1, row_devs):
        peer = lax.rem(r + d, row_devs)
        rights.append(
            remote(
                gr_ref.at[peer], buf_r.at[d - 1], r_send.at[d - 1], r_recv.at[d - 1], {"row": peer}
            )
        )
    for d in range(1, count):
        peer, where = place(d)
        outs.append(
            remote(gw_ref.at[peer], buf_w.at[d - 1], w_send.at[d - 1], w_recv.at[d - 1], where)
        )
    for copy in rights + lefts + outs:
        copy.start()

    for copy in rights:
        copy.wait_recv()
    total = gr_ref[r].astype(f32)
    for d in range(1, row_devs):
        total = total + buf_r[d - 1].astype(f32)
    done_r[...] = total.astype(bf16)

    def right_copy(k, d):
        return remote(
            done_r.at[k],
            out_r.at[r],
            r2_send.at[k * col_devs + d],
            r2_recv.at[r],
            {"row": c * ratio + k, "col": lax.rem(c + d, col_devs)},
        )

    for k in range(ratio):
        for d in range(1, col_devs):
            right_copy(k, d).start()

        @pl.when(c * ratio + k == r)
        def _():
            out_r[r] = done_r[k]

        @pl.when(c * ratio + k != r)
        def _():
            right_copy(k, 0).start()

    for copy in lefts:
        copy.wait_recv()
    total = gl_ref[c].astype(f32)
    for d in range(1, col_devs):
        total = total + buf_l[d - 1].astype(f32)
    done_l[...] = total.astype(bf16)
    left_copies = []
    for d in range(1, col_devs):
        left_copies.append(
            remote(
                done_l,
                out_l.at[c],
                l2_send.at[d - 1],
                l2_recv.at[d - 1],
                {"col": lax.rem(c + d, col_devs)},
            )
        )
    for copy in left_copies:
        copy.start()
    out_l[c] = done_l[...]

    for copy in outs:
        copy.wait_recv()
    total = gw_ref[me].astype(f32)
    for d in range(1, count):
        total = total + buf_w[d - 1].astype(f32)
    out_w[...] = total * scale

    for copy in left_copies:
        copy.wait_recv()
    for src in range(row_devs):
        own = jnp.logical_and(r == src, c == r // ratio)

        @pl.when(jnp.logical_not(own))
        def _():
            remote(
                done_r.at[0], out_r.at[src], r2_send.at[0], r2_recv.at[src], {"col": c}
            ).wait_recv()

    for copy in rights + lefts + outs + left_copies:
        copy.wait_send()
    for k in range(ratio):
        for d in range(1, col_devs):
            right_copy(k, d).wait_send()

        @pl.when(c * ratio + k != r)
        def _():
            right_copy(k, 0).wait_send()


def device_sums(gl, gr, gw, row_devs, col_devs, ratio, scale):
    count = row_devs * col_devs
    dma = pltpu.SemaphoreType.DMA
    return pl.pallas_call(
        functools.partial(sums_kernel, row_devs, col_devs, ratio, scale),
        out_shape=(
            jax.ShapeDtypeStruct(gl.shape, bf16),
            jax.ShapeDtypeStruct((row_devs,) + gr.shape[2:], bf16),
            jax.ShapeDtypeStruct(gw.shape[1:], f32),
        ),
        in_specs=[VMEM] * 3,
        out_specs=(VMEM,) * 3,
        scratch_shapes=[
            pltpu.VMEM((col_devs - 1,) + gl.shape[1:], bf16),
            pltpu.VMEM((row_devs - 1,) + gr.shape[1:], bf16),
            pltpu.VMEM((count - 1,) + gw.shape[1:], bf16),
            pltpu.VMEM(gl.shape[1:], bf16),
            pltpu.VMEM(gr.shape[1:], bf16),
            dma((col_devs - 1,)),
            dma((col_devs - 1,)),
            dma((row_devs - 1,)),
            dma((row_devs - 1,)),
            dma((count - 1,)),
            dma((count - 1,)),
            dma((col_devs - 1,)),
            dma((col_devs - 1,)),
            dma((ratio * col_devs,)),
            dma((row_devs,)),
        ],
        compiler_params=pltpu.CompilerParams(
            collective_id=1, has_side_effects=True, vmem_limit_bytes=32 * 1024 * 1024
        ),
        name="device_sums",
    )(gl, gr, gw)


def weights_kernel(row_devs, scale, own_ref, out_ref, buf, send_sem, recv_sem):
    r = lax.axis_index("row")
    barrier = pltpu.get_barrier_semaphore()
    for d in range(1, row_devs):
        pl.semaphore_signal(
            barrier, inc=1, device_id={"row": lax.rem(r + d, row_devs)}, device_id_type=MESH
        )
    pl.semaphore_wait(barrier, row_devs - 1)
    copies = []
    for d in range(1, row_devs):
        copies.append(
            pltpu.make_async_remote_copy(
                src_ref=own_ref,
                dst_ref=buf.at[r],
                send_sem=send_sem.at[d - 1],
                recv_sem=recv_sem.at[d - 1],
                device_id={"row": lax.rem(r + d, row_devs)},
                device_id_type=MESH,
            )
        )
    for copy in copies:
        copy.start()
    buf[r] = own_ref[...]
    for copy in copies:
        copy.wait_recv()
    total = buf[0]
    for src in range(1, row_devs):
        total = total + buf[src]
    out_ref[...] = total * scale
    for copy in copies:
        copy.wait_send()


def sum_weights(own, row_devs, scale):
    return pl.pallas_call(
        functools.partial(weights_kernel, row_devs, scale),
        out_shape=jax.ShapeDtypeStruct(own.shape, f32),
        in_specs=[VMEM],
        out_specs=VMEM,
        scratch_shapes=[
            pltpu.VMEM((row_devs,) + own.shape, f32),
            pltpu.SemaphoreType.DMA((row_devs - 1,)),
            pltpu.SemaphoreType.DMA((row_devs - 1,)),
        ],
        compiler_params=pltpu.CompilerParams(collective_id=2, has_side_effects=True),
        name="sum_weights",
    )(own)


def body(
    alignment_activations,
    sequence_presence_flags,
    residue_padding_mask,
    left_weight,
    right_weight,
    output_weight,
    cotangent,
):
    row_idx = lax.axis_index("row")
    col_idx = lax.axis_index("col")
    row_devs = lax.axis_size("row")
    col_devs = lax.axis_size("col")
    ratio = row_devs // col_devs
    seqs, residues, channels = alignment_activations.shape
    residue_total = sequence_presence_flags.shape[1]
    cols = residue_total // col_devs
    width = left_weight.shape[1]
    z = output_weight.shape[1]
    count = row_devs * col_devs

    active_mask = (sequence_presence_flags * residue_padding_mask[None, :]).astype(f32)
    own_live = lax.dynamic_slice_in_dim(active_mask, row_idx * residues, residues, 1)
    live_cols = lax.dynamic_slice_in_dim(active_mask, col_idx * cols, cols, 1)
    unit, inverse_deviation = layer_normalize(alignment_activations)
    normed = unit.astype(bf16)
    right_own = jnp.einsum("snd,de->sen", normed, right_weight, preferred_element_type=f32)
    right_own = (right_own * own_live[:, None, :]).astype(bf16).reshape(seqs, width * residues)
    right = spread_right(right_own, row_devs, ratio)
    right = right.reshape(ratio, seqs, width, residues).transpose(1, 2, 0, 3)
    right = right.reshape(seqs, width * cols)
    left = jnp.einsum("snd,dc->snc", normed, left_weight, preferred_element_type=f32)
    left = (left * own_live[..., None]).astype(bf16).reshape(seqs, residues * width)
    divisor = jnp.maximum(jnp.dot(own_live.T, live_cols, precision=lax.Precision.HIGHEST), 1.0)
    live_left = jnp.repeat(own_live.astype(bf16), width, axis=1)
    live_right = jnp.tile(live_cols.astype(bf16), (1, width))

    pair, gl, gr, gw = pair_block(
        left, right, divisor, cotangent, output_weight, live_left, live_right, width
    )

    gl = gl.reshape(col_devs, 16, -1)
    gr = gr.reshape(row_devs, seqs // row_devs, width, ratio, residues)
    gr = gr.transpose(0, 3, 1, 2, 4).reshape(row_devs, ratio, 16, -1)
    per = gw.shape[1] // z
    gw = gw.reshape(width // per, width, per, z).transpose(1, 0, 2, 3)
    gw = gw.reshape(count, width * width // count, z)
    grad_left, grad_right, out_share = device_sums(
        gl, gr, gw, row_devs, col_devs, ratio, 1.0 / residue_total
    )
    grad_left = grad_left.reshape(seqs, residues, width)
    grad_right = grad_right.reshape(seqs, width, residues).transpose(0, 2, 1)
    grads = jnp.concatenate([grad_left, grad_right], -1)
    weights = jnp.concatenate([left_weight, right_weight], -1)
    wgrad = jnp.einsum("snd,snc->dc", normed, grads, preferred_element_type=f32)
    wgrad = sum_weights(wgrad, row_devs, 1.0 / residue_total)
    grad_normed = jnp.einsum("snc,dc->snd", grads, weights, preferred_element_type=f32)
    centered = (
        grad_normed
        - jnp.mean(grad_normed, -1, keepdims=True)
        - unit * jnp.mean(grad_normed * unit, -1, keepdims=True)
    )
    alignment_gradient = (inverse_deviation * centered).astype(bf16)
    return (pair, alignment_gradient, out_share, wgrad[:, :width], wgrad[:, width:])


def solution(mesh):
    return jax.shard_map(
        body,
        mesh=mesh,
        in_specs=(
            P("crop", "row", None),
            P("crop", None),
            P("crop"),
            P(),
            P(),
            P(),
            P(("crop", "row"), "col", None),
        ),
        out_specs=(
            P(("crop", "row"), "col", None),
            P("crop", "row", None),
            P(("crop", "row", "col"), None),
            P("crop", None),
            P("crop", None),
        ),
        check_vma=False,
    )
```

```python
import functools

import jax
import jax.numpy as jnp
from jax import lax
from jax.experimental import pallas as pl
from jax.experimental.pallas import tpu as pltpu
from jax.sharding import PartitionSpec as P

norm_eps = 1e-05
MESH = pl.DeviceIdType.MESH
NT = (((1,), (1,)), ((), ()))
TN = (((0,), (0,)), ((), ()))
VMEM = pl.BlockSpec(memory_space=pltpu.VMEM)
f32 = jnp.float32
bf16 = jnp.bfloat16


def layer_normalize(values):
    floats = values.astype(jnp.float32)
    average = jnp.mean(floats, -1, keepdims=True)
    centred = floats - average
    variance = jnp.mean(centred * centred, -1, keepdims=True)
    inverse_deviation = lax.rsqrt(variance + norm_eps)
    return (centred * inverse_deviation, inverse_deviation)


def pairs_kernel(
    row_devs,
    col_devs,
    ib,
    width,
    scale,
    own_ref,
    left_ref,
    div_ref,
    cot_ref,
    wst_ref,
    wst2_ref,
    live_left_ref,
    live_right_ref,
    pair_ref,
    out_l,
    out_r,
    out_w,
    got,
    right_ref,
    x_ref,
    s_ref,
    gp_ref,
    gw_acc,
    gl_ref,
    gr_ref,
    gw_ref,
    buf_l,
    buf_r,
    buf_w,
    done_l,
    done_r,
    a_send,
    a_recv,
    l_send,
    l_recv,
    r_send,
    r_recv,
    w_send,
    w_recv,
    l2_send,
    l2_recv,
    r2_send,
    r2_recv,
):
    r = lax.axis_index("row")
    c = lax.axis_index("col")
    ratio = row_devs // col_devs
    count = row_devs * col_devs
    me = r * col_devs + c
    rows, cols, z = cot_ref.shape
    seqs = left_ref.shape[0]
    per = wst_ref.shape[0] // z
    tile = per * cols
    groups = width // per
    steps = rows // ib
    residues = cols // ratio

    def place(d):
        peer = lax.rem(me + d, count)
        return peer, {"row": peer // col_devs, "col": lax.rem(peer, col_devs)}

    def remote(src, dst, send, recv, where):
        return pltpu.make_async_remote_copy(
            src_ref=src,
            dst_ref=dst,
            send_sem=send,
            recv_sem=recv,
            device_id=where,
            device_id_type=MESH,
        )

    barrier = pltpu.get_barrier_semaphore()
    for d in range(1, count):
        pl.semaphore_signal(barrier, inc=1, device_id=place(d)[1], device_id_type=MESH)
    pl.semaphore_wait(barrier, count - 1)

    def spread(k, d):
        where = {"row": lax.rem(r + d, row_devs)}
        return remote(own_ref, got.at[k], a_send.at[d], a_recv.at[k], where)

    for k in range(ratio):

        @pl.when(c * ratio + k == r)
        def _():
            for d in range(1, row_devs):
                spread(k, d).start()
            got[k] = own_ref[...]

    def grad_step(b, carry):
        inverse = 1.0 / div_ref[b]
        base = pl.multiple_of(b * (ib * tile), ib * tile)
        for i in range(ib):
            scaled = (cot_ref[b * ib + i].astype(f32) * inverse[:, i : i + 1]).astype(bf16)
            for p in range(per):
                at = pl.ds(base + i * tile + p * cols, cols)
                for q in range(per):
                    s_ref[at, q * z : (q + 1) * z] = scaled if p == q else jnp.zeros_like(scaled)
        block = s_ref[pl.ds(base, ib * tile)]
        first = pl.multiple_of(b * (ib * width), ib * width)
        for g in range(groups):
            part = slice(g * width, (g + 1) * width)
            go = lax.dot_general(wst2_ref[part], block, NT, preferred_element_type=f32)
            go = go.astype(bf16)
            for i in range(ib):
                gp_ref[pl.ds(first + i * width, width), g * tile : (g + 1) * tile] = go[
                    :, i * tile : (i + 1) * tile
                ]
        return carry

    lax.fori_loop(0, steps, grad_step, 0)

    for k in range(ratio):

        @pl.when(c * ratio + k != r)
        def _():
            spread(k, 1).wait_recv()

    if ratio == 1:
        right_ref[...] = got[0]
    else:
        for k in range(ratio):
            for e in range(width):
                at = e * cols + k * residues
                right_ref[:, at : at + residues] = got[k, :, e * residues : (e + 1) * residues]

    wide = 256
    slab = seqs // row_devs
    for n in range(0, cols * width, wide):
        gr = jnp.dot(left_ref[...], gp_ref[:, n : n + wide], preferred_element_type=f32)
        gr = (gr * live_right_ref[:, n : n + wide].astype(f32)).astype(bf16)
        for src in range(row_devs):
            piece = gr[src * slab : (src + 1) * slab]
            if ratio == 1:
                gr_ref[src, 0, :, n : n + wide] = piece
            else:
                for o in range(0, wide, residues):
                    e, k = (n + o) // cols, (n + o) % cols // residues
                    gr_ref[src, k, :, e * residues : (e + 1) * residues] = piece[:, o : o + residues]
    rights = []
    for d in range(1, row_devs):
        peer = lax.rem(r + d, row_devs)
        rights.append(
            remote(
                gr_ref.at[peer], buf_r.at[d - 1], r_send.at[d - 1], r_recv.at[d - 1], {"row": peer}
            )
        )
    for copy in rights:
        copy.start()

    slab_l = seqs // col_devs
    for n in range(0, rows * width, wide):
        gl = lax.dot_general(
            right_ref[...], gp_ref[n : n + wide], NT, preferred_element_type=f32
        )
        gl = (gl * live_left_ref[:, n : n + wide].astype(f32)).astype(bf16)
        for src in range(col_devs):
            gl_ref[src, :, n : n + wide] = gl[src * slab_l : (src + 1) * slab_l]
    lefts = []
    for d in range(1, col_devs):
        peer = lax.rem(c + d, col_devs)
        lefts.append(
            remote(
                gl_ref.at[peer], buf_l.at[d - 1], l_send.at[d - 1], l_recv.at[d - 1], {"col": peer}
            )
        )
    for copy in lefts:
        copy.start()

    gw_acc[...] = jnp.zeros_like(gw_acc)
    lanes = lax.broadcasted_iota(jnp.int32, (z, tile), 1)

    def pair_step(b, carry):
        left = left_ref[:, pl.ds(pl.multiple_of(b * (ib * width), ib * width), ib * width)]
        for g in range(groups):
            part = lax.dot_general(
                left, right_ref[:, g * tile : (g + 1) * tile], TN, preferred_element_type=f32
            ).astype(bf16)
            for i in range(ib):
                x_ref[g * width : (g + 1) * width, i * tile : (i + 1) * tile] = part[
                    i * width : (i + 1) * width
                ]
        inverse = 1.0 / div_ref[b]
        for i in range(ib):
            sl = slice(i * tile, (i + 1) * tile)
            y = jnp.dot(wst_ref[...], x_ref[:, sl], preferred_element_type=f32)
            picked = y[:z]
            for p in range(1, per):
                picked = jnp.where(lanes < p * cols, picked, y[p * z : (p + 1) * z])
            turned = picked.T
            total = turned[:cols]
            for p in range(1, per):
                total = total + turned[p * cols : (p + 1) * cols]
            pair_ref[b * ib + i] = (total * inverse[:, i : i + 1]).astype(bf16)
        block = s_ref[pl.ds(pl.multiple_of(b * (ib * tile), ib * tile), ib * tile)]
        share = jnp.dot(x_ref[...], block, preferred_element_type=f32)
        gw_acc[...] += share.reshape(groups, width, per * z)
        return carry

    lax.fori_loop(0, steps // 2, pair_step, 0)

    for copy in rights:
        copy.wait_recv()
    total = gr_ref[r].astype(f32)
    for d in range(1, row_devs):
        total = total + buf_r[d - 1].astype(f32)
    done_r[...] = total.astype(bf16)

    def right_copy(k, d):
        return remote(
            done_r.at[k],
            out_r.at[r],
            r2_send.at[k * col_devs + d],
            r2_recv.at[r],
            {"row": c * ratio + k, "col": lax.rem(c + d, col_devs)},
        )

    for k in range(ratio):
        for d in range(1, col_devs):
            right_copy(k, d).start()

        @pl.when(c * ratio + k == r)
        def _():
            out_r[r] = done_r[k]

        @pl.when(c * ratio + k != r)
        def _():
            right_copy(k, 0).start()

    for copy in lefts:
        copy.wait_recv()
    total = gl_ref[c].astype(f32)
    for d in range(1, col_devs):
        total = total + buf_l[d - 1].astype(f32)
    done_l[...] = total.astype(bf16)
    left_copies = []
    for d in range(1, col_devs):
        where = {"col": lax.rem(c + d, col_devs)}
        left_copies.append(
            remote(done_l, out_l.at[c], l2_send.at[d - 1], l2_recv.at[d - 1], where)
        )
    for copy in left_copies:
        copy.start()
    out_l[c] = done_l[...]

    lax.fori_loop(steps // 2, steps, pair_step, 0)

    chunk = out_w.shape[0]
    piece = min(groups, chunk)
    for ch in range(width):
        row = gw_acc[:, ch, :].astype(bf16)
        for p in range(per):
            for o in range(0, groups, piece):
                flat = (ch * per + p) * groups + o
                at = flat % chunk
                gw_ref[flat // chunk, at : at + piece] = row[o : o + piece, p * z : (p + 1) * z]
    outs = []
    for d in range(1, count):
        peer, where = place(d)
        outs.append(
            remote(gw_ref.at[peer], buf_w.at[d - 1], w_send.at[d - 1], w_recv.at[d - 1], where)
        )
    for copy in outs:
        copy.start()

    for copy in left_copies:
        copy.wait_recv()
    for src in range(row_devs):
        own = jnp.logical_and(r == src, c == r // ratio)

        @pl.when(jnp.logical_not(own))
        def _():
            where = {"col": lax.rem(c + 1, col_devs)}
            remote(
                done_r.at[0], out_r.at[src], r2_send.at[0], r2_recv.at[src], where
            ).wait_recv()

    for copy in outs:
        copy.wait_recv()
    total = gw_ref[me].astype(f32)
    for d in range(1, count):
        total = total + buf_w[d - 1].astype(f32)
    total = total * scale
    if per == 1:
        out_w[...] = total
    else:
        for o in range(0, chunk, groups):
            ch, p = o // groups // per, o // groups % per
            out_w[pl.ds(ch * width + p, groups, stride=per), :] = total[o : o + groups]

    for copy in rights + lefts + outs + left_copies:
        copy.wait_send()
    for k in range(ratio):

        @pl.when(c * ratio + k == r)
        def _():
            for d in range(1, row_devs):
                spread(k, d).wait_send()

        for d in range(1, col_devs):
            right_copy(k, d).wait_send()

        @pl.when(c * ratio + k != r)
        def _():
            right_copy(k, 0).wait_send()


def pairs(
    own, left, divisor, cotangent, weight, live_left, live_right, width, row_devs, col_devs, scale
):
    rows, cols, z = cotangent.shape
    seqs = left.shape[0]
    ib = 8
    steps = rows // ib
    per = max(1, 128 // cols)
    tile = per * cols
    groups = width // per
    ratio = row_devs // col_devs
    count = row_devs * col_devs
    residues = cols // ratio
    chunk = width * width // count
    wst2 = weight.reshape(width, groups, per, z).transpose(1, 0, 2, 3)
    wst2 = wst2.reshape(groups * width, per * z)
    div = divisor.reshape(steps, ib, cols).transpose(0, 2, 1)
    dma = pltpu.SemaphoreType.DMA
    vmem = pltpu.VMEM
    l_shape = (seqs // col_devs, rows * width)
    r_shape = (seqs // row_devs, residues * width)
    return pl.pallas_call(
        functools.partial(pairs_kernel, row_devs, col_devs, ib, width, scale),
        out_shape=(
            jax.ShapeDtypeStruct((rows, cols, z), bf16),
            jax.ShapeDtypeStruct((col_devs,) + l_shape, bf16),
            jax.ShapeDtypeStruct((row_devs,) + r_shape, bf16),
            jax.ShapeDtypeStruct((chunk, z), f32),
        ),
        in_specs=[VMEM] * 8,
        out_specs=(VMEM,) * 4,
        scratch_shapes=[
            vmem((ratio, seqs, residues * width), bf16),
            vmem((seqs, cols * width), bf16),
            vmem((groups * width, ib * tile), bf16),
            vmem((rows * tile, per * z), bf16),
            vmem((rows * width, groups * tile), bf16),
            vmem((groups, width, per * z), f32),
            vmem((col_devs,) + l_shape, bf16),
            vmem((row_devs, ratio) + r_shape, bf16),
            vmem((count, chunk, z), bf16),
            vmem((col_devs - 1,) + l_shape, bf16),
            vmem((row_devs - 1, ratio) + r_shape, bf16),
            vmem((count - 1, chunk, z), bf16),
            vmem(l_shape, bf16),
            vmem((ratio,) + r_shape, bf16),
            dma((row_devs,)),
            dma((ratio,)),
            dma((col_devs - 1,)),
            dma((col_devs - 1,)),
            dma((row_devs - 1,)),
            dma((row_devs - 1,)),
            dma((count - 1,)),
            dma((count - 1,)),
            dma((col_devs - 1,)),
            dma((col_devs - 1,)),
            dma((ratio * col_devs,)),
            dma((row_devs,)),
        ],
        compiler_params=pltpu.CompilerParams(
            collective_id=0, has_side_effects=True, vmem_limit_bytes=52 * 1024 * 1024
        ),
        name="pairs",
    )(own, left, div, cotangent, wst2.T, wst2, live_left, live_right)


def tail_kernel(
    row_devs,
    scale,
    x_ref,
    grads_ref,
    weights_ref,
    align_ref,
    left_ref,
    right_ref,
    buf,
    unit_ref,
    inv_ref,
    send_sem,
    recv_sem,
):
    r = lax.axis_index("row")
    rows = 512
    steps = x_ref.shape[0] // rows
    barrier = pltpu.get_barrier_semaphore()
    for d in range(1, row_devs):
        where = {"row": lax.rem(r + d, row_devs)}
        pl.semaphore_signal(barrier, inc=1, device_id=where, device_id_type=MESH)

    def weight_step(b, total):
        at = pl.ds(pl.multiple_of(b * rows, rows), rows)
        unit, inverse = layer_normalize(x_ref[at])
        unit_ref[at] = unit
        inv_ref[at] = inverse
        return total + lax.dot_general(
            grads_ref[at], unit.astype(bf16), TN, preferred_element_type=f32
        )

    total = lax.fori_loop(0, steps, weight_step, jnp.zeros(buf.shape[1:], f32))
    buf[r] = total
    pl.semaphore_wait(barrier, row_devs - 1)
    copies = []
    for d in range(1, row_devs):
        copies.append(
            pltpu.make_async_remote_copy(
                src_ref=buf.at[r],
                dst_ref=buf.at[r],
                send_sem=send_sem.at[d - 1],
                recv_sem=recv_sem.at[d - 1],
                device_id={"row": lax.rem(r + d, row_devs)},
                device_id_type=MESH,
            )
        )
    for copy in copies:
        copy.start()

    def input_step(b, carry):
        at = pl.ds(pl.multiple_of(b * rows, rows), rows)
        unit = unit_ref[at]
        grad = lax.dot_general(grads_ref[at], weights_ref[...], NT, preferred_element_type=f32)
        grad = (
            grad
            - jnp.mean(grad, -1, keepdims=True)
            - unit * jnp.mean(grad * unit, -1, keepdims=True)
        )
        align_ref[at] = (inv_ref[at] * grad).astype(bf16)
        return carry

    lax.fori_loop(0, steps, input_step, 0)
    for d in range(1, row_devs):
        src = lax.rem(r - d + row_devs, row_devs)
        pltpu.make_async_remote_copy(
            src_ref=buf.at[src],
            dst_ref=buf.at[src],
            send_sem=send_sem.at[d - 1],
            recv_sem=recv_sem.at[d - 1],
            device_id={"row": lax.rem(r + d, row_devs)},
            device_id_type=MESH,
        ).wait_recv()
    total = buf[0]
    for src in range(1, row_devs):
        total = total + buf[src]
    total = (total * scale).T
    width = left_ref.shape[1]
    left_ref[...] = total[:, :width]
    right_ref[...] = total[:, width:]
    for copy in copies:
        copy.wait_send()


def tail(x, grads, weights, row_devs, scale):
    rows, channels = x.shape
    both = grads.shape[1]
    width = both // 2
    return pl.pallas_call(
        functools.partial(tail_kernel, row_devs, scale),
        out_shape=(
            jax.ShapeDtypeStruct(x.shape, bf16),
            jax.ShapeDtypeStruct((channels, width), f32),
            jax.ShapeDtypeStruct((channels, width), f32),
        ),
        in_specs=[VMEM] * 3,
        out_specs=(VMEM,) * 3,
        scratch_shapes=[
            pltpu.VMEM((row_devs, both, channels), f32),
            pltpu.VMEM((rows, channels), f32),
            pltpu.VMEM((rows, 1), f32),
            pltpu.SemaphoreType.DMA((row_devs - 1,)),
            pltpu.SemaphoreType.DMA((row_devs - 1,)),
        ],
        compiler_params=pltpu.CompilerParams(
            collective_id=1, has_side_effects=True, vmem_limit_bytes=48 * 1024 * 1024
        ),
        name="tail",
    )(x, grads, weights)


def body(
    alignment_activations,
    sequence_presence_flags,
    residue_padding_mask,
    left_weight,
    right_weight,
    output_weight,
    cotangent,
):
    row_idx = lax.axis_index("row")
    col_idx = lax.axis_index("col")
    row_devs = lax.axis_size("row")
    col_devs = lax.axis_size("col")
    seqs, residues, channels = alignment_activations.shape
    residue_total = sequence_presence_flags.shape[1]
    cols = residue_total // col_devs
    width = left_weight.shape[1]

    active_mask = (sequence_presence_flags * residue_padding_mask[None, :]).astype(f32)
    own_live = lax.dynamic_slice_in_dim(active_mask, row_idx * residues, residues, 1)
    live_cols = lax.dynamic_slice_in_dim(active_mask, col_idx * cols, cols, 1)
    unit, _ = layer_normalize(alignment_activations)
    normed = unit.astype(bf16)
    right_own = jnp.einsum("snd,de->sen", normed, right_weight, preferred_element_type=f32)
    right_own = (right_own * own_live[:, None, :]).astype(bf16).reshape(seqs, width * residues)
    left = jnp.einsum("snd,dc->snc", normed, left_weight, preferred_element_type=f32)
    left = (left * own_live[..., None]).astype(bf16).reshape(seqs, residues * width)
    divisor = jnp.maximum(jnp.dot(own_live.T, live_cols, precision=lax.Precision.HIGHEST), 1.0)
    live_left = jnp.repeat(own_live.astype(bf16), width, axis=1)
    live_right = jnp.tile(live_cols.astype(bf16), (1, width))

    pair, grad_left, grad_right, out_share = pairs(
        right_own,
        left,
        divisor,
        cotangent,
        output_weight,
        live_left,
        live_right,
        width,
        row_devs,
        col_devs,
        1.0 / residue_total,
    )
    grad_left = grad_left.reshape(seqs, residues, width)
    grad_right = grad_right.reshape(seqs, width, residues).transpose(0, 2, 1)
    grads = jnp.concatenate([grad_left, grad_right], -1).reshape(seqs * residues, 2 * width)
    weights = jnp.concatenate([left_weight, right_weight], -1)
    flat = alignment_activations.reshape(seqs * residues, channels)
    align, left_wgrad, right_wgrad = tail(flat, grads, weights, row_devs, 1.0 / residue_total)
    align = align.reshape(seqs, residues, channels)
    return (pair, align, out_share, left_wgrad, right_wgrad)


def solution(mesh):
    return jax.shard_map(
        body,
        mesh=mesh,
        in_specs=(
            P("crop", "row", None),
            P("crop", None),
            P("crop"),
            P(),
            P(),
            P(),
            P(("crop", "row"), "col", None),
        ),
        out_specs=(
            P(("crop", "row"), "col", None),
            P("crop", "row", None),
            P(("crop", "row", "col"), None),
            P("crop", None),
            P("crop", None),
        ),
        check_vma=False,
    )
```

```python
import functools

import jax
import jax.numpy as jnp
from jax import lax
from jax.experimental import pallas as pl
from jax.experimental.pallas import tpu as pltpu
from jax.sharding import PartitionSpec as P

norm_eps = 1e-05
MESH = pl.DeviceIdType.MESH
NT = (((1,), (1,)), ((), ()))
TN = (((0,), (0,)), ((), ()))
VMEM = pl.BlockSpec(memory_space=pltpu.VMEM)
f32 = jnp.float32
bf16 = jnp.bfloat16


def layer_normalize(values):
    floats = values.astype(jnp.float32)
    average = jnp.mean(floats, -1, keepdims=True)
    centred = floats - average
    variance = jnp.mean(centred * centred, -1, keepdims=True)
    inverse_deviation = lax.rsqrt(variance + norm_eps)
    return (centred * inverse_deviation, inverse_deviation)


def pairs_kernel(
    row_devs,
    col_devs,
    ib,
    width,
    scale,
    own_ref,
    left_ref,
    div_ref,
    cot_ref,
    wst_ref,
    wst2_ref,
    pair_ref,
    out_l,
    out_r,
    out_w,
    got,
    right_ref,
    x_ref,
    s_ref,
    gp_ref,
    gw_acc,
    gl_ref,
    gr_ref,
    gw_ref,
    buf_l,
    buf_r,
    buf_w,
    done_l,
    done_r,
    a_send,
    a_recv,
    l_send,
    l_recv,
    r_send,
    r_recv,
    w_send,
    w_recv,
    l2_send,
    l2_recv,
    r2_send,
    r2_recv,
):
    r = lax.axis_index("row")
    c = lax.axis_index("col")
    ratio = row_devs // col_devs
    count = row_devs * col_devs
    me = r * col_devs + c
    rows, cols, z = cot_ref.shape
    seqs = left_ref.shape[0]
    per = wst_ref.shape[0] // z
    tile = per * cols
    groups = width // per
    steps = rows // ib
    residues = cols // ratio

    def place(d):
        peer = lax.rem(me + d, count)
        return peer, {"row": peer // col_devs, "col": lax.rem(peer, col_devs)}

    def remote(src, dst, send, recv, where):
        return pltpu.make_async_remote_copy(
            src_ref=src,
            dst_ref=dst,
            send_sem=send,
            recv_sem=recv,
            device_id=where,
            device_id_type=MESH,
        )

    barrier = pltpu.get_barrier_semaphore()
    for d in range(1, count):
        pl.semaphore_signal(barrier, inc=1, device_id=place(d)[1], device_id_type=MESH)
    pl.semaphore_wait(barrier, count - 1)

    def spread(k, d):
        where = {"row": lax.rem(r + d, row_devs)}
        return remote(own_ref, got.at[k], a_send.at[d], a_recv.at[k], where)

    for k in range(ratio):

        @pl.when(c * ratio + k == r)
        def _():
            for d in range(1, row_devs):
                spread(k, d).start()
            got[k] = own_ref[...]

    def grad_step(b, carry):
        inverse = 1.0 / div_ref[b]
        base = pl.multiple_of(b * (ib * tile), ib * tile)
        for i in range(ib):
            scaled = (cot_ref[b * ib + i].astype(f32) * inverse[:, i : i + 1]).astype(bf16)
            for p in range(per):
                at = pl.ds(base + i * tile + p * cols, cols)
                for q in range(per):
                    s_ref[at, q * z : (q + 1) * z] = scaled if p == q else jnp.zeros_like(scaled)
        block = s_ref[pl.ds(base, ib * tile)]
        first = pl.multiple_of(b * (ib * width), ib * width)
        for g in range(groups):
            part = slice(g * width, (g + 1) * width)
            go = lax.dot_general(wst2_ref[part], block, NT, preferred_element_type=f32)
            go = go.astype(bf16)
            for i in range(ib):
                gp_ref[pl.ds(first + i * width, width), g * tile : (g + 1) * tile] = go[
                    :, i * tile : (i + 1) * tile
                ]
        return carry

    lax.fori_loop(0, steps, grad_step, 0)

    for k in range(ratio):

        @pl.when(c * ratio + k != r)
        def _():
            spread(k, 1).wait_recv()

    if ratio == 1:
        right_ref[...] = got[0]
    else:
        for k in range(ratio):
            for e in range(width):
                at = e * cols + k * residues
                right_ref[:, at : at + residues] = got[k, :, e * residues : (e + 1) * residues]

    wide = 256
    slab_l = seqs // col_devs
    for n in range(0, rows * width, wide):
        gl = lax.dot_general(
            right_ref[...], gp_ref[n : n + wide], NT, preferred_element_type=f32
        )
        gl = gl.astype(bf16)
        for src in range(col_devs):
            gl_ref[src, :, n : n + wide] = gl[src * slab_l : (src + 1) * slab_l]
    lefts = []
    for d in range(1, col_devs):
        peer = lax.rem(c + d, col_devs)
        lefts.append(
            remote(
                gl_ref.at[peer], buf_l.at[d - 1], l_send.at[d - 1], l_recv.at[d - 1], {"col": peer}
            )
        )
    for copy in lefts:
        copy.start()

    slab = seqs // row_devs
    for n in range(0, cols * width, wide):
        gr = jnp.dot(left_ref[...], gp_ref[:, n : n + wide], preferred_element_type=f32)
        gr = gr.astype(bf16)
        for src in range(row_devs):
            piece = gr[src * slab : (src + 1) * slab]
            if ratio == 1:
                gr_ref[src, 0, :, n : n + wide] = piece
            else:
                for o in range(0, wide, residues):
                    e, k = (n + o) // cols, (n + o) % cols // residues
                    gr_ref[src, k, :, e * residues : (e + 1) * residues] = piece[:, o : o + residues]
    rights = []
    for d in range(1, row_devs):
        peer = lax.rem(r + d, row_devs)
        rights.append(
            remote(
                gr_ref.at[peer], buf_r.at[d - 1], r_send.at[d - 1], r_recv.at[d - 1], {"row": peer}
            )
        )
    for copy in rights:
        copy.start()

    gw_acc[...] = jnp.zeros_like(gw_acc)
    lanes = lax.broadcasted_iota(jnp.int32, (z, tile), 1)

    def outer_step(b, carry):
        left = left_ref[:, pl.ds(pl.multiple_of(b * (ib * width), ib * width), ib * width)]
        at = pl.ds(pl.multiple_of(b * (ib * tile), ib * tile), ib * tile)
        for g in range(groups):
            part = lax.dot_general(
                left, right_ref[:, g * tile : (g + 1) * tile], TN, preferred_element_type=f32
            ).astype(bf16)
            for i in range(ib):
                x_ref[b, g * width : (g + 1) * width, i * tile : (i + 1) * tile] = part[
                    i * width : (i + 1) * width
                ]
        share = jnp.dot(x_ref[b], s_ref[at], preferred_element_type=f32)
        gw_acc[...] += share.reshape(groups, width, per * z)
        return carry

    def pair_step(b, carry):
        inverse = 1.0 / div_ref[b]
        for i in range(ib):
            sl = slice(i * tile, (i + 1) * tile)
            y = jnp.dot(wst_ref[...], x_ref[b, :, sl], preferred_element_type=f32)
            picked = y[:z]
            for p in range(1, per):
                picked = jnp.where(lanes < p * cols, picked, y[p * z : (p + 1) * z])
            turned = picked.T
            total = turned[:cols]
            for p in range(1, per):
                total = total + turned[p * cols : (p + 1) * cols]
            pair_ref[b * ib + i] = (total * inverse[:, i : i + 1]).astype(bf16)
        return carry

    lax.fori_loop(0, steps // 2, outer_step, 0)

    for copy in rights:
        copy.wait_recv()
    total = gr_ref[r].astype(f32)
    for d in range(1, row_devs):
        total = total + buf_r[d - 1].astype(f32)
    done_r[...] = total.astype(bf16)

    def right_copy(k, d):
        return remote(
            done_r.at[k],
            out_r.at[r],
            r2_send.at[k * col_devs + d],
            r2_recv.at[r],
            {"row": c * ratio + k, "col": lax.rem(c + d, col_devs)},
        )

    for k in range(ratio):
        for d in range(1, col_devs):
            right_copy(k, d).start()

        @pl.when(c * ratio + k == r)
        def _():
            out_r[r] = done_r[k]

        @pl.when(c * ratio + k != r)
        def _():
            right_copy(k, 0).start()

    for copy in lefts:
        copy.wait_recv()
    total = gl_ref[c].astype(f32)
    for d in range(1, col_devs):
        total = total + buf_l[d - 1].astype(f32)
    done_l[...] = total.astype(bf16)
    left_copies = []
    for d in range(1, col_devs):
        where = {"col": lax.rem(c + d, col_devs)}
        left_copies.append(
            remote(done_l, out_l.at[c], l2_send.at[d - 1], l2_recv.at[d - 1], where)
        )
    for copy in left_copies:
        copy.start()
    out_l[c] = done_l[...]

    lax.fori_loop(steps // 2, steps, outer_step, 0)

    chunk = out_w.shape[0]
    piece = min(groups, chunk)
    for ch in range(width):
        row = gw_acc[:, ch, :].astype(bf16)
        for p in range(per):
            for o in range(0, groups, piece):
                flat = (ch * per + p) * groups + o
                at = flat % chunk
                gw_ref[flat // chunk, at : at + piece] = row[o : o + piece, p * z : (p + 1) * z]
    outs = []
    for d in range(1, count):
        peer, where = place(d)
        outs.append(
            remote(gw_ref.at[peer], buf_w.at[d - 1], w_send.at[d - 1], w_recv.at[d - 1], where)
        )
    for copy in outs:
        copy.start()

    lax.fori_loop(0, steps, pair_step, 0)

    for copy in left_copies:
        copy.wait_recv()
    for src in range(row_devs):
        own = jnp.logical_and(r == src, c == r // ratio)

        @pl.when(jnp.logical_not(own))
        def _():
            where = {"col": lax.rem(c + 1, col_devs)}
            remote(
                done_r.at[0], out_r.at[src], r2_send.at[0], r2_recv.at[src], where
            ).wait_recv()

    for copy in outs:
        copy.wait_recv()
    total = gw_ref[me].astype(f32)
    for d in range(1, count):
        total = total + buf_w[d - 1].astype(f32)
    total = total * scale
    if per == 1:
        out_w[...] = total
    else:
        for o in range(0, chunk, groups):
            ch, p = o // groups // per, o // groups % per
            out_w[pl.ds(ch * width + p, groups, stride=per), :] = total[o : o + groups]

    for copy in rights + lefts + outs + left_copies:
        copy.wait_send()
    for k in range(ratio):

        @pl.when(c * ratio + k == r)
        def _():
            for d in range(1, row_devs):
                spread(k, d).wait_send()

        for d in range(1, col_devs):
            right_copy(k, d).wait_send()

        @pl.when(c * ratio + k != r)
        def _():
            right_copy(k, 0).wait_send()


def pairs(
    own, left, divisor, cotangent, weight, width, row_devs, col_devs, scale
):
    rows, cols, z = cotangent.shape
    seqs = left.shape[0]
    ib = 8
    steps = rows // ib
    per = max(1, 128 // cols)
    tile = per * cols
    groups = width // per
    ratio = row_devs // col_devs
    count = row_devs * col_devs
    residues = cols // ratio
    chunk = width * width // count
    wst2 = weight.reshape(width, groups, per, z).transpose(1, 0, 2, 3)
    wst2 = wst2.reshape(groups * width, per * z)
    div = divisor.reshape(steps, ib, cols).transpose(0, 2, 1)
    dma = pltpu.SemaphoreType.DMA
    vmem = pltpu.VMEM
    l_shape = (seqs // col_devs, rows * width)
    r_shape = (seqs // row_devs, residues * width)
    return pl.pallas_call(
        functools.partial(pairs_kernel, row_devs, col_devs, ib, width, scale),
        out_shape=(
            jax.ShapeDtypeStruct((rows, cols, z), bf16),
            jax.ShapeDtypeStruct((col_devs,) + l_shape, bf16),
            jax.ShapeDtypeStruct((row_devs,) + r_shape, bf16),
            jax.ShapeDtypeStruct((chunk, z), f32),
        ),
        in_specs=[VMEM] * 6,
        out_specs=(VMEM,) * 4,
        scratch_shapes=[
            vmem((ratio, seqs, residues * width), bf16),
            vmem((seqs, cols * width), bf16),
            vmem((steps, groups * width, ib * tile), bf16),
            vmem((rows * tile, per * z), bf16),
            vmem((rows * width, groups * tile), bf16),
            vmem((groups, width, per * z), f32),
            vmem((col_devs,) + l_shape, bf16),
            vmem((row_devs, ratio) + r_shape, bf16),
            vmem((count, chunk, z), bf16),
            vmem((col_devs - 1,) + l_shape, bf16),
            vmem((row_devs - 1, ratio) + r_shape, bf16),
            vmem((count - 1, chunk, z), bf16),
            vmem(l_shape, bf16),
            vmem((ratio,) + r_shape, bf16),
            dma((row_devs,)),
            dma((ratio,)),
            dma((col_devs - 1,)),
            dma((col_devs - 1,)),
            dma((row_devs - 1,)),
            dma((row_devs - 1,)),
            dma((count - 1,)),
            dma((count - 1,)),
            dma((col_devs - 1,)),
            dma((col_devs - 1,)),
            dma((ratio * col_devs,)),
            dma((row_devs,)),
        ],
        compiler_params=pltpu.CompilerParams(
            collective_id=0, has_side_effects=True, vmem_limit_bytes=52 * 1024 * 1024
        ),
        name="pairs",
    )(own, left, div, cotangent, wst2.T, wst2)


def tail_kernel(
    row_devs,
    x_ref,
    grads_ref,
    weights_ref,
    align_ref,
    out_ref,
    buf,
    unit_ref,
    inv_ref,
    send_sem,
    recv_sem,
):
    r = lax.axis_index("row")
    rows = 512
    steps = x_ref.shape[0] // rows
    barrier = pltpu.get_barrier_semaphore()
    for d in range(1, row_devs):
        where = {"row": lax.rem(r + d, row_devs)}
        pl.semaphore_signal(barrier, inc=1, device_id=where, device_id_type=MESH)

    def weight_step(b, total):
        at = pl.ds(pl.multiple_of(b * rows, rows), rows)
        unit, inverse = layer_normalize(x_ref[at])
        unit_ref[at] = unit
        inv_ref[at] = inverse
        return total + lax.dot_general(
            grads_ref[at], unit.astype(bf16), TN, preferred_element_type=f32
        )

    total = lax.fori_loop(0, steps, weight_step, jnp.zeros(buf.shape[1:], f32))
    buf[r] = total
    pl.semaphore_wait(barrier, row_devs - 1)
    copies = []
    for d in range(1, row_devs):
        copies.append(
            pltpu.make_async_remote_copy(
                src_ref=buf.at[r],
                dst_ref=buf.at[r],
                send_sem=send_sem.at[d - 1],
                recv_sem=recv_sem.at[d - 1],
                device_id={"row": lax.rem(r + d, row_devs)},
                device_id_type=MESH,
            )
        )
    for copy in copies:
        copy.start()

    def input_step(b, carry):
        at = pl.ds(pl.multiple_of(b * rows, rows), rows)
        unit = unit_ref[at]
        grad = lax.dot_general(grads_ref[at], weights_ref[...], NT, preferred_element_type=f32)
        grad = (
            grad
            - jnp.mean(grad, -1, keepdims=True)
            - unit * jnp.mean(grad * unit, -1, keepdims=True)
        )
        align_ref[at] = (inv_ref[at] * grad).astype(bf16)
        return carry

    lax.fori_loop(0, steps, input_step, 0)
    for d in range(1, row_devs):
        src = lax.rem(r - d + row_devs, row_devs)
        pltpu.make_async_remote_copy(
            src_ref=buf.at[src],
            dst_ref=buf.at[src],
            send_sem=send_sem.at[d - 1],
            recv_sem=recv_sem.at[d - 1],
            device_id={"row": lax.rem(r + d, row_devs)},
            device_id_type=MESH,
        ).wait_recv()
    total = buf[0]
    for src in range(1, row_devs):
        total = total + buf[src]
    out_ref[...] = total
    for copy in copies:
        copy.wait_send()


def tail(x, grads, weights, row_devs):
    rows, channels = x.shape
    both = grads.shape[1]
    return pl.pallas_call(
        functools.partial(tail_kernel, row_devs),
        out_shape=(
            jax.ShapeDtypeStruct(x.shape, bf16),
            jax.ShapeDtypeStruct((both, channels), f32),
        ),
        in_specs=[VMEM] * 3,
        out_specs=(VMEM,) * 2,
        scratch_shapes=[
            pltpu.VMEM((row_devs, both, channels), f32),
            pltpu.VMEM((rows, channels), f32),
            pltpu.VMEM((rows, 1), f32),
            pltpu.SemaphoreType.DMA((row_devs - 1,)),
            pltpu.SemaphoreType.DMA((row_devs - 1,)),
        ],
        compiler_params=pltpu.CompilerParams(
            collective_id=1, has_side_effects=True, vmem_limit_bytes=48 * 1024 * 1024
        ),
        name="tail",
    )(x, grads, weights)


def body(
    alignment_activations,
    sequence_presence_flags,
    residue_padding_mask,
    left_weight,
    right_weight,
    output_weight,
    cotangent,
):
    row_idx = lax.axis_index("row")
    col_idx = lax.axis_index("col")
    row_devs = lax.axis_size("row")
    col_devs = lax.axis_size("col")
    seqs, residues, channels = alignment_activations.shape
    residue_total = sequence_presence_flags.shape[1]
    cols = residue_total // col_devs
    width = left_weight.shape[1]

    active_mask = (sequence_presence_flags * residue_padding_mask[None, :]).astype(f32)
    own_live = lax.dynamic_slice_in_dim(active_mask, row_idx * residues, residues, 1)
    live_cols = lax.dynamic_slice_in_dim(active_mask, col_idx * cols, cols, 1)
    unit, _ = layer_normalize(alignment_activations)
    normed = unit.astype(bf16)
    right_own = jnp.einsum("snd,de->sen", normed, right_weight, preferred_element_type=f32)
    right_own = (right_own * own_live[:, None, :]).astype(bf16).reshape(seqs, width * residues)
    left = jnp.einsum("snd,dc->snc", normed, left_weight, preferred_element_type=f32)
    left = (left * own_live[..., None]).astype(bf16).reshape(seqs, residues * width)
    divisor = jnp.maximum(jnp.dot(own_live.T, live_cols, precision=lax.Precision.HIGHEST), 1.0)

    pair, grad_left, grad_right, out_share = pairs(
        right_own,
        left,
        divisor,
        cotangent,
        output_weight,
        width,
        row_devs,
        col_devs,
        1.0 / residue_total,
    )
    grad_left = grad_left.reshape(seqs, residues, width)
    grad_right = grad_right.reshape(seqs, width, residues).transpose(0, 2, 1)
    grads = jnp.concatenate([grad_left, grad_right], -1) * own_live.astype(bf16)[..., None]
    grads = grads.reshape(seqs * residues, 2 * width)
    weights = jnp.concatenate([left_weight, right_weight], -1)
    flat = alignment_activations.reshape(seqs * residues, channels)
    align, wgrad = tail(flat, grads, weights, row_devs)
    left_wgrad = wgrad[:width].T / residue_total
    right_wgrad = wgrad[width:].T / residue_total
    align = align.reshape(seqs, residues, channels)
    return (pair, align, out_share, left_wgrad, right_wgrad)


def solution(mesh):
    return jax.shard_map(
        body,
        mesh=mesh,
        in_specs=(
            P("crop", "row", None),
            P("crop", None),
            P("crop"),
            P(),
            P(),
            P(),
            P(("crop", "row"), "col", None),
        ),
        out_specs=(
            P(("crop", "row"), "col", None),
            P("crop", "row", None),
            P(("crop", "row", "col"), None),
            P("crop", None),
            P("crop", None),
        ),
        check_vma=False,
    )
```

```python
import functools

import jax
import jax.numpy as jnp
from jax import lax
from jax.experimental import pallas as pl
from jax.experimental.pallas import tpu as pltpu
from jax.sharding import PartitionSpec as P

norm_eps = 1e-05
MESH = pl.DeviceIdType.MESH
NT = (((1,), (1,)), ((), ()))
TN = (((0,), (0,)), ((), ()))
VMEM = pl.BlockSpec(memory_space=pltpu.VMEM)
f32 = jnp.float32
bf16 = jnp.bfloat16


def layer_normalize(values):
    floats = values.astype(jnp.float32)
    average = jnp.mean(floats, -1, keepdims=True)
    centred = floats - average
    variance = jnp.mean(centred * centred, -1, keepdims=True)
    inverse_deviation = lax.rsqrt(variance + norm_eps)
    return (centred * inverse_deviation, inverse_deviation)


def pairs_kernel(
    row_devs,
    col_devs,
    ib,
    width,
    scale,
    own_ref,
    left_ref,
    div_ref,
    cot_ref,
    wst_ref,
    wst2_ref,
    pair_ref,
    out_l,
    out_r,
    out_w,
    got,
    right_ref,
    x_ref,
    s_ref,
    gp_ref,
    gw_acc,
    gl_ref,
    gr_ref,
    gw_ref,
    buf_l,
    buf_r,
    buf_w,
    buf_v,
    done_w,
    done_l,
    done_r,
    a_send,
    a_recv,
    l_send,
    l_recv,
    r_send,
    r_recv,
    w_send,
    w_recv,
    v_send,
    v_recv,
    l2_send,
    l2_recv,
    r2_send,
    r2_recv,
):
    r = lax.axis_index("row")
    c = lax.axis_index("col")
    ratio = row_devs // col_devs
    count = row_devs * col_devs
    me = r * col_devs + c
    rows, cols, z = cot_ref.shape
    seqs = left_ref.shape[0]
    per = wst_ref.shape[0] // z
    tile = per * cols
    groups = width // per
    steps = rows // ib
    residues = cols // ratio

    def place(d):
        peer = lax.rem(me + d, count)
        return peer, {"row": peer // col_devs, "col": lax.rem(peer, col_devs)}

    def remote(src, dst, send, recv, where):
        return pltpu.make_async_remote_copy(
            src_ref=src,
            dst_ref=dst,
            send_sem=send,
            recv_sem=recv,
            device_id=where,
            device_id_type=MESH,
        )

    barrier = pltpu.get_barrier_semaphore()
    for d in range(1, count):
        pl.semaphore_signal(barrier, inc=1, device_id=place(d)[1], device_id_type=MESH)
    pl.semaphore_wait(barrier, count - 1)

    def spread(k, d):
        where = {"row": lax.rem(r + d, row_devs)}
        return remote(own_ref, got.at[k], a_send.at[d], a_recv.at[k], where)

    for k in range(ratio):

        @pl.when(c * ratio + k == r)
        def _():
            for d in range(1, row_devs):
                spread(k, d).start()
            got[k] = own_ref[...]

    def grad_step(b, carry):
        inverse = 1.0 / div_ref[b]
        base = pl.multiple_of(b * (ib * tile), ib * tile)
        for i in range(ib):
            scaled = (cot_ref[b * ib + i].astype(f32) * inverse[:, i : i + 1]).astype(bf16)
            for p in range(per):
                at = pl.ds(base + i * tile + p * cols, cols)
                for q in range(per):
                    s_ref[at, q * z : (q + 1) * z] = scaled if p == q else jnp.zeros_like(scaled)
        block = s_ref[pl.ds(base, ib * tile)]
        first = pl.multiple_of(b * (ib * width), ib * width)
        for g in range(groups):
            part = slice(g * width, (g + 1) * width)
            go = lax.dot_general(wst2_ref[part], block, NT, preferred_element_type=f32)
            go = go.astype(bf16)
            for i in range(ib):
                gp_ref[pl.ds(first + i * width, width), g * tile : (g + 1) * tile] = go[
                    :, i * tile : (i + 1) * tile
                ]
        return carry

    lax.fori_loop(0, steps, grad_step, 0)

    for k in range(ratio):

        @pl.when(c * ratio + k != r)
        def _():
            spread(k, 1).wait_recv()

    if ratio == 1:
        right_ref[...] = got[0]
    else:
        for k in range(ratio):
            for e in range(width):
                at = e * cols + k * residues
                right_ref[:, at : at + residues] = got[k, :, e * residues : (e + 1) * residues]

    wide = 256
    slab_l = seqs // col_devs
    for n in range(0, rows * width, wide):
        gl = lax.dot_general(
            right_ref[...], gp_ref[n : n + wide], NT, preferred_element_type=f32
        )
        gl = gl.astype(bf16)
        for src in range(col_devs):
            gl_ref[src, :, n : n + wide] = gl[src * slab_l : (src + 1) * slab_l]
    lefts = []
    for d in range(1, col_devs):
        peer = lax.rem(c + d, col_devs)
        lefts.append(
            remote(
                gl_ref.at[peer], buf_l.at[d - 1], l_send.at[d - 1], l_recv.at[d - 1], {"col": peer}
            )
        )
    for copy in lefts:
        copy.start()

    slab = seqs // row_devs
    for n in range(0, cols * width, wide):
        gr = jnp.dot(left_ref[...], gp_ref[:, n : n + wide], preferred_element_type=f32)
        gr = gr.astype(bf16)
        for src in range(row_devs):
            piece = gr[src * slab : (src + 1) * slab]
            if ratio == 1:
                gr_ref[src, 0, :, n : n + wide] = piece
            else:
                for o in range(0, wide, residues):
                    e, k = (n + o) // cols, (n + o) % cols // residues
                    gr_ref[src, k, :, e * residues : (e + 1) * residues] = piece[:, o : o + residues]
    rights = []
    for d in range(1, row_devs):
        peer = lax.rem(r + d, row_devs)
        rights.append(
            remote(
                gr_ref.at[peer], buf_r.at[d - 1], r_send.at[d - 1], r_recv.at[d - 1], {"row": peer}
            )
        )
    for copy in rights:
        copy.start()

    gw_acc[...] = jnp.zeros_like(gw_acc)
    lanes = lax.broadcasted_iota(jnp.int32, (z, tile), 1)

    def outer_step(b, carry):
        left = left_ref[:, pl.ds(pl.multiple_of(b * (ib * width), ib * width), ib * width)]
        at = pl.ds(pl.multiple_of(b * (ib * tile), ib * tile), ib * tile)
        for g in range(groups):
            part = lax.dot_general(
                left, right_ref[:, g * tile : (g + 1) * tile], TN, preferred_element_type=f32
            ).astype(bf16)
            for i in range(ib):
                x_ref[b, g * width : (g + 1) * width, i * tile : (i + 1) * tile] = part[
                    i * width : (i + 1) * width
                ]
        share = jnp.dot(x_ref[b], s_ref[at], preferred_element_type=f32)
        gw_acc[...] += share.reshape(groups, width, per * z)
        return carry

    def pair_step(b, carry):
        inverse = 1.0 / div_ref[b]
        for i in range(ib):
            sl = slice(i * tile, (i + 1) * tile)
            y = jnp.dot(wst_ref[...], x_ref[b, :, sl], preferred_element_type=f32)
            picked = y[:z]
            for p in range(1, per):
                picked = jnp.where(lanes < p * cols, picked, y[p * z : (p + 1) * z])
            turned = picked.T
            total = turned[:cols]
            for p in range(1, per):
                total = total + turned[p * cols : (p + 1) * cols]
            pair_ref[b * ib + i] = (total * inverse[:, i : i + 1]).astype(bf16)
        return carry

    lax.fori_loop(0, steps // 2, outer_step, 0)

    for copy in rights:
        copy.wait_recv()
    total = gr_ref[r].astype(f32)
    for d in range(1, row_devs):
        total = total + buf_r[d - 1].astype(f32)
    done_r[...] = total.astype(bf16)

    def right_copy(k, d):
        return remote(
            done_r.at[k],
            out_r.at[r],
            r2_send.at[k * col_devs + d],
            r2_recv.at[r],
            {"row": c * ratio + k, "col": lax.rem(c + d, col_devs)},
        )

    for k in range(ratio):
        for d in range(1, col_devs):
            right_copy(k, d).start()

        @pl.when(c * ratio + k == r)
        def _():
            out_r[r] = done_r[k]

        @pl.when(c * ratio + k != r)
        def _():
            right_copy(k, 0).start()

    for copy in lefts:
        copy.wait_recv()
    total = gl_ref[c].astype(f32)
    for d in range(1, col_devs):
        total = total + buf_l[d - 1].astype(f32)
    done_l[...] = total.astype(bf16)
    left_copies = []
    for d in range(1, col_devs):
        where = {"col": lax.rem(c + d, col_devs)}
        left_copies.append(
            remote(done_l, out_l.at[c], l2_send.at[d - 1], l2_recv.at[d - 1], where)
        )
    for copy in left_copies:
        copy.start()
    out_l[c] = done_l[...]

    lax.fori_loop(steps // 2, steps, outer_step, 0)

    chunk = out_w.shape[0]
    piece = min(groups, chunk)
    for ch in range(width):
        row = gw_acc[:, ch, :].astype(bf16)
        for p in range(per):
            for o in range(0, groups, piece):
                flat = (ch * per + p) * groups + o
                at = flat % chunk
                gw_ref[flat // chunk, at : at + piece] = row[o : o + piece, p * z : (p + 1) * z]
    outs = []
    for d in range(1, row_devs):
        peer = lax.rem(r + d, row_devs)
        part = gw_ref.at[pl.ds(peer * col_devs, col_devs)]
        outs.append(
            remote(part, buf_w.at[d - 1], w_send.at[d - 1], w_recv.at[d - 1], {"row": peer})
        )
    for copy in outs:
        copy.start()

    lax.fori_loop(0, steps // 2, pair_step, 0)

    for copy in outs:
        copy.wait_recv()
    total = gw_ref[pl.ds(r * col_devs, col_devs)].astype(f32)
    for d in range(1, row_devs):
        total = total + buf_w[d - 1].astype(f32)
    done_w[...] = total.astype(bf16)
    out_copies = []
    for d in range(1, col_devs):
        peer = lax.rem(c + d, col_devs)
        out_copies.append(
            remote(
                done_w.at[peer], buf_v.at[d - 1], v_send.at[d - 1], v_recv.at[d - 1], {"col": peer}
            )
        )
    for copy in out_copies:
        copy.start()

    lax.fori_loop(steps // 2, steps, pair_step, 0)

    for copy in left_copies:
        copy.wait_recv()
    for src in range(row_devs):
        own = jnp.logical_and(r == src, c == r // ratio)

        @pl.when(jnp.logical_not(own))
        def _():
            where = {"col": lax.rem(c + 1, col_devs)}
            remote(
                done_r.at[0], out_r.at[src], r2_send.at[0], r2_recv.at[src], where
            ).wait_recv()

    for copy in out_copies:
        copy.wait_recv()
    total = done_w[c].astype(f32)
    for d in range(1, col_devs):
        total = total + buf_v[d - 1].astype(f32)
    total = total * scale
    if per == 1:
        out_w[...] = total
    else:
        for o in range(0, chunk, groups):
            ch, p = o // groups // per, o // groups % per
            out_w[pl.ds(ch * width + p, groups, stride=per), :] = total[o : o + groups]

    for copy in rights + lefts + outs + left_copies + out_copies:
        copy.wait_send()
    for k in range(ratio):

        @pl.when(c * ratio + k == r)
        def _():
            for d in range(1, row_devs):
                spread(k, d).wait_send()

        for d in range(1, col_devs):
            right_copy(k, d).wait_send()

        @pl.when(c * ratio + k != r)
        def _():
            right_copy(k, 0).wait_send()


def pairs(
    own, left, divisor, cotangent, weight, width, row_devs, col_devs, scale
):
    rows, cols, z = cotangent.shape
    seqs = left.shape[0]
    ib = 8
    steps = rows // ib
    per = max(1, 128 // cols)
    tile = per * cols
    groups = width // per
    ratio = row_devs // col_devs
    count = row_devs * col_devs
    residues = cols // ratio
    chunk = width * width // count
    wst2 = weight.reshape(width, groups, per, z).transpose(1, 0, 2, 3)
    wst2 = wst2.reshape(groups * width, per * z)
    div = divisor.reshape(steps, ib, cols).transpose(0, 2, 1)
    dma = pltpu.SemaphoreType.DMA
    vmem = pltpu.VMEM
    l_shape = (seqs // col_devs, rows * width)
    r_shape = (seqs // row_devs, residues * width)
    return pl.pallas_call(
        functools.partial(pairs_kernel, row_devs, col_devs, ib, width, scale),
        out_shape=(
            jax.ShapeDtypeStruct((rows, cols, z), bf16),
            jax.ShapeDtypeStruct((col_devs,) + l_shape, bf16),
            jax.ShapeDtypeStruct((row_devs,) + r_shape, bf16),
            jax.ShapeDtypeStruct((chunk, z), f32),
        ),
        in_specs=[VMEM] * 6,
        out_specs=(VMEM,) * 4,
        scratch_shapes=[
            vmem((ratio, seqs, residues * width), bf16),
            vmem((seqs, cols * width), bf16),
            vmem((steps, groups * width, ib * tile), bf16),
            vmem((rows * tile, per * z), bf16),
            vmem((rows * width, groups * tile), bf16),
            vmem((groups, width, per * z), f32),
            vmem((col_devs,) + l_shape, bf16),
            vmem((row_devs, ratio) + r_shape, bf16),
            vmem((count, chunk, z), bf16),
            vmem((col_devs - 1,) + l_shape, bf16),
            vmem((row_devs - 1, ratio) + r_shape, bf16),
            vmem((row_devs - 1, col_devs, chunk, z), bf16),
            vmem((col_devs - 1, chunk, z), bf16),
            vmem((col_devs, chunk, z), bf16),
            vmem(l_shape, bf16),
            vmem((ratio,) + r_shape, bf16),
            dma((row_devs,)),
            dma((ratio,)),
            dma((col_devs - 1,)),
            dma((col_devs - 1,)),
            dma((row_devs - 1,)),
            dma((row_devs - 1,)),
            dma((row_devs - 1,)),
            dma((row_devs - 1,)),
            dma((col_devs - 1,)),
            dma((col_devs - 1,)),
            dma((col_devs - 1,)),
            dma((col_devs - 1,)),
            dma((ratio * col_devs,)),
            dma((row_devs,)),
        ],
        compiler_params=pltpu.CompilerParams(
            collective_id=0, has_side_effects=True, vmem_limit_bytes=52 * 1024 * 1024
        ),
        name="pairs",
    )(own, left, div, cotangent, wst2.T, wst2)


def tail_kernel(
    row_devs,
    x_ref,
    grads_ref,
    weights_ref,
    align_ref,
    out_ref,
    buf,
    unit_ref,
    inv_ref,
    send_sem,
    recv_sem,
):
    r = lax.axis_index("row")
    rows = 512
    steps = x_ref.shape[0] // rows
    barrier = pltpu.get_barrier_semaphore()
    for d in range(1, row_devs):
        where = {"row": lax.rem(r + d, row_devs)}
        pl.semaphore_signal(barrier, inc=1, device_id=where, device_id_type=MESH)

    def weight_step(b, total):
        at = pl.ds(pl.multiple_of(b * rows, rows), rows)
        unit, inverse = layer_normalize(x_ref[at])
        unit_ref[at] = unit
        inv_ref[at] = inverse
        return total + lax.dot_general(
            grads_ref[at], unit.astype(bf16), TN, preferred_element_type=f32
        )

    total = lax.fori_loop(0, steps, weight_step, jnp.zeros(buf.shape[1:], f32))
    buf[r] = total
    pl.semaphore_wait(barrier, row_devs - 1)
    copies = []
    for d in range(1, row_devs):
        copies.append(
            pltpu.make_async_remote_copy(
                src_ref=buf.at[r],
                dst_ref=buf.at[r],
                send_sem=send_sem.at[d - 1],
                recv_sem=recv_sem.at[d - 1],
                device_id={"row": lax.rem(r + d, row_devs)},
                device_id_type=MESH,
            )
        )
    for copy in copies:
        copy.start()

    def input_step(b, carry):
        at = pl.ds(pl.multiple_of(b * rows, rows), rows)
        unit = unit_ref[at]
        grad = lax.dot_general(grads_ref[at], weights_ref[...], NT, preferred_element_type=f32)
        grad = (
            grad
            - jnp.mean(grad, -1, keepdims=True)
            - unit * jnp.mean(grad * unit, -1, keepdims=True)
        )
        align_ref[at] = (inv_ref[at] * grad).astype(bf16)
        return carry

    lax.fori_loop(0, steps, input_step, 0)
    for d in range(1, row_devs):
        src = lax.rem(r - d + row_devs, row_devs)
        pltpu.make_async_remote_copy(
            src_ref=buf.at[src],
            dst_ref=buf.at[src],
            send_sem=send_sem.at[d - 1],
            recv_sem=recv_sem.at[d - 1],
            device_id={"row": lax.rem(r + d, row_devs)},
            device_id_type=MESH,
        ).wait_recv()
    total = buf[0]
    for src in range(1, row_devs):
        total = total + buf[src]
    out_ref[...] = total
    for copy in copies:
        copy.wait_send()


def tail(x, grads, weights, row_devs):
    rows, channels = x.shape
    both = grads.shape[1]
    return pl.pallas_call(
        functools.partial(tail_kernel, row_devs),
        out_shape=(
            jax.ShapeDtypeStruct(x.shape, bf16),
            jax.ShapeDtypeStruct((both, channels), f32),
        ),
        in_specs=[VMEM] * 3,
        out_specs=(VMEM,) * 2,
        scratch_shapes=[
            pltpu.VMEM((row_devs, both, channels), f32),
            pltpu.VMEM((rows, channels), f32),
            pltpu.VMEM((rows, 1), f32),
            pltpu.SemaphoreType.DMA((row_devs - 1,)),
            pltpu.SemaphoreType.DMA((row_devs - 1,)),
        ],
        compiler_params=pltpu.CompilerParams(
            collective_id=1, has_side_effects=True, vmem_limit_bytes=48 * 1024 * 1024
        ),
        name="tail",
    )(x, grads, weights)


def body(
    alignment_activations,
    sequence_presence_flags,
    residue_padding_mask,
    left_weight,
    right_weight,
    output_weight,
    cotangent,
):
    row_idx = lax.axis_index("row")
    col_idx = lax.axis_index("col")
    row_devs = lax.axis_size("row")
    col_devs = lax.axis_size("col")
    seqs, residues, channels = alignment_activations.shape
    residue_total = sequence_presence_flags.shape[1]
    cols = residue_total // col_devs
    width = left_weight.shape[1]

    active_mask = (sequence_presence_flags * residue_padding_mask[None, :]).astype(f32)
    own_live = lax.dynamic_slice_in_dim(active_mask, row_idx * residues, residues, 1)
    live_cols = lax.dynamic_slice_in_dim(active_mask, col_idx * cols, cols, 1)
    unit, _ = layer_normalize(alignment_activations)
    normed = unit.astype(bf16)
    right_own = jnp.einsum("snd,de->sen", normed, right_weight, preferred_element_type=f32)
    right_own = (right_own * own_live[:, None, :]).astype(bf16).reshape(seqs, width * residues)
    left = jnp.einsum("snd,dc->snc", normed, left_weight, preferred_element_type=f32)
    left = (left * own_live[..., None]).astype(bf16).reshape(seqs, residues * width)
    divisor = jnp.maximum(jnp.dot(own_live.T, live_cols, precision=lax.Precision.HIGHEST), 1.0)

    pair, grad_left, grad_right, out_share = pairs(
        right_own,
        left,
        divisor,
        cotangent,
        output_weight,
        width,
        row_devs,
        col_devs,
        1.0 / residue_total,
    )
    grad_left = grad_left.reshape(seqs, residues, width)
    grad_right = grad_right.reshape(seqs, width, residues).transpose(0, 2, 1)
    grads = jnp.concatenate([grad_left, grad_right], -1) * own_live.astype(bf16)[..., None]
    grads = grads.reshape(seqs * residues, 2 * width)
    weights = jnp.concatenate([left_weight, right_weight], -1)
    flat = alignment_activations.reshape(seqs * residues, channels)
    align, wgrad = tail(flat, grads, weights, row_devs)
    left_wgrad = wgrad[:width].T / residue_total
    right_wgrad = wgrad[width:].T / residue_total
    align = align.reshape(seqs, residues, channels)
    return (pair, align, out_share, left_wgrad, right_wgrad)


def solution(mesh):
    return jax.shard_map(
        body,
        mesh=mesh,
        in_specs=(
            P("crop", "row", None),
            P("crop", None),
            P("crop"),
            P(),
            P(),
            P(),
            P(("crop", "row"), "col", None),
        ),
        out_specs=(
            P(("crop", "row"), "col", None),
            P("crop", "row", None),
            P(("crop", "row", "col"), None),
            P("crop", None),
            P("crop", None),
        ),
        check_vma=False,
    )
```
